32 devices in a mesh: dp: 8 (over z, x), tensor: 4 (over y, core).
Axes of the slice: x: 2, y: 2, z: 4, core: 2. Of those that a mesh axis runs over, the one named last changes fastest.
Arguments:
- gate_preactivation: bfloat16 [128, 28672], P('dp', 'tensor'), may hold values from -6 to 6
- up_preactivation: bfloat16 [128, 28672], P('dp', 'tensor'), may hold values from -6 to 6
- cotangent: bfloat16 [128, 8192], P('dp'), may hold values from -0.5 to 0.5
- down_weight: bfloat16 [28672, 8192], P('tensor', 'dp'), may hold values from -0.03125 to 0.03125
- lowrank_factor_first: bfloat16 [28672, 64], P('tensor'), may hold values from -0.03125 to 0.03125
- lowrank_factor_second: bfloat16 [64, 8192], replicated, may hold values from -0.75 to 0.75
- sparse_block_values: bfloat16 [8, 4, 2, 128, 128], P('dp', 'tensor'), may hold values from -0.5 to 0.5
- slot_block_rows: int32 [8, 4, 2], P(None, 'tensor'), may hold values from 0 to 55, as said below
- slot_block_columns: int32 [8, 4, 2], P(None, 'tensor'), may hold values from 0 to 7
- owner_slot_counts: int32 [8, 4], P(None, 'tensor'), may hold values from 1 to 2, as said below
Outputs:
- mixed: bfloat16 [128, 8192], P('tensor', 'dp')
- grad_a: float32 [28672, 64], P('tensor')
- grad_b: float32 [64, 8192], P(None, 'dp')
- grad_blocks: float32 [8, 4, 2, 128, 128], P('dp', 'tensor')
The draws below stay inside these ranges and needn't reach their ends.
Inputs may be any that keep to these rules, and one draw needn't show every extreme that they name: `slot_block_rows`: the 2 slots of one owner name different blocks. `owner_slot_counts`: some owner has exactly 2 live slots.
All inputs are finite; a program needn't handle non-finite values.
Results may differ from the reference program's by a relative error of at most 0.0049.
Values may be sent and summed in bfloat16 or wider, within the bound.
A program may use at most 128 MiB of HBM per device.

```python
import jax
import jax.numpy as jnp
from jax import lax

MODEL_WIDTH = 8192
HIDDEN_UNITS = 28672
ADAPTER_RANK = 64
BS = 128
CAP = 2
TOKENS = 128
N_DP = 8
N_TENSOR = 4


def block_choice(key):
    inner = jax.random.fold_in(key, 11)
    spots = HIDDEN_UNITS // N_TENSOR // BS * (MODEL_WIDTH // N_DP // BS)
    scores = jax.random.randint(inner, (N_DP, N_TENSOR, spots), 0, 1 << 20) * spots + jnp.arange(spots, dtype=jnp.int32)
    return jnp.argsort(scores, axis=-1)[..., :CAP].astype(jnp.int32)


def draw_slot_block_rows(key, part):
    return (block_choice(key) // (MODEL_WIDTH // N_DP // BS)).astype(jnp.int32)


def draw_slot_block_columns(key, part):
    return (block_choice(key) % (MODEL_WIDTH // N_DP // BS)).astype(jnp.int32)


def draw_owner_slot_counts(key, part):
    counts = jax.random.randint(jax.random.fold_in(key, 23), (N_DP * N_TENSOR,), 1, CAP + 1)
    spot = jax.random.randint(jax.random.fold_in(key, 29), (), 0, N_DP * N_TENSOR)
    counts = jnp.where(jnp.arange(N_DP * N_TENSOR, dtype=jnp.int32) == spot, CAP, counts)
    return counts.reshape(N_DP, N_TENSOR).astype(jnp.int32)


def block_levels(own_key, shape, shards, low, top_value):
    level = 1.0
    for axis_at, blocks in shards:
        steps = jax.random.uniform(jax.random.fold_in(jax.random.fold_in(own_key, 6), axis_at), (blocks,), jnp.float32, low / len(shards), top_value / len(shards))
        level = level * jnp.repeat(jnp.exp(steps), shape[axis_at] // blocks).reshape((-1,) + (1,) * (len(shape) - 1 - axis_at))
    return level


def bell_draw(stream_key, shape, scale, reach, pieces=(), kind=jnp.bfloat16):
    loudness = block_levels(stream_key, shape, pieces, -0.22, 0.18) if pieces else 1.0
    drawn = jax.random.normal(stream_key, shape, jnp.float32) * scale * loudness
    return jnp.minimum(jnp.maximum(drawn, -reach), reach).astype(kind)


def setup_inputs(seed: int = 0) -> dict:
    seeds = jax.random.split(jax.random.key(seed), 11)
    return {
        "gate_preactivation": bell_draw(seeds[0], (TOKENS, HIDDEN_UNITS), 1.0, 6.0, ((0, 8), (1, 4))),
        "up_preactivation": bell_draw(seeds[1], (TOKENS, HIDDEN_UNITS), 1.0, 6.0, ((0, 8), (1, 4))),
        "cotangent": bell_draw(seeds[2], (TOKENS, MODEL_WIDTH), (TOKENS ** -0.5), 0.5, ((0, 8),)),
        "down_weight": bell_draw(seeds[3], (HIDDEN_UNITS, MODEL_WIDTH), HIDDEN_UNITS ** -0.5, 0.03125, ((0, 4), (1, 8))),
        "lowrank_factor_first": bell_draw(seeds[4], (HIDDEN_UNITS, ADAPTER_RANK), HIDDEN_UNITS ** -0.5, 0.03125, ((0, 4),)),
        "lowrank_factor_second": bell_draw(seeds[5], (ADAPTER_RANK, MODEL_WIDTH), ADAPTER_RANK ** -0.5, 0.75),
        "sparse_block_values": bell_draw(seeds[6], (N_DP, N_TENSOR, CAP, BS, BS), BS ** -0.5, 0.5, ((0, 8), (1, 4))),
        "slot_block_rows": draw_slot_block_rows(jax.random.fold_in(seeds[10], 71), 0),
        "slot_block_columns": draw_slot_block_columns(jax.random.fold_in(seeds[10], 71), 0),
        "owner_slot_counts": draw_owner_slot_counts(jax.random.fold_in(seeds[10], 71), 0),
    }


def reference(gate_preactivation, up_preactivation, cotangent, down_weight, lowrank_factor_first, lowrank_factor_second, sparse_block_values, slot_block_rows, slot_block_columns, owner_slot_counts):
    hidden_activation = (jax.nn.silu(gate_preactivation.astype(jnp.float32)) * up_preactivation.astype(jnp.float32)).astype(jnp.bfloat16)
    lowrank_projection = jnp.dot(hidden_activation, lowrank_factor_first, preferred_element_type=jnp.float32)
    frozen_product = jnp.dot(hidden_activation, down_weight, preferred_element_type=jnp.float32)
    frozen_product = frozen_product + jnp.dot(lowrank_projection, lowrank_factor_second.astype(jnp.float32), precision=lax.Precision.HIGHEST)
    per_row = HIDDEN_UNITS // N_TENSOR // BS
    per_col = MODEL_WIDTH // N_DP // BS
    live = (jnp.arange(CAP, dtype=jnp.int32)[None, None, :] < owner_slot_counts[:, :, None]).astype(jnp.float32)
    global_rows = (jnp.arange(N_TENSOR, dtype=jnp.int32)[None, :, None] * per_row + slot_block_rows).astype(jnp.int32)
    picked = jnp.take(hidden_activation.reshape(TOKENS, HIDDEN_UNITS // BS, BS), global_rows.reshape(-1), axis=1)
    picked = picked.reshape(TOKENS, N_DP, N_TENSOR, CAP, BS).astype(jnp.float32)
    local = jnp.einsum("tojkc,ojkcd->tojkd", picked, sparse_block_values.astype(jnp.float32), precision=lax.Precision.HIGHEST)
    col_pick = (slot_block_columns[..., None] == jnp.arange(per_col, dtype=jnp.int32)).astype(jnp.float32)
    spread = jnp.einsum("tojkd,ojkn->tond", local, col_pick * live[..., None], precision=lax.Precision.HIGHEST)
    mixed = (frozen_product + spread.reshape(TOKENS, MODEL_WIDTH)).astype(jnp.bfloat16)
    cotangent_lowrank = lax.dot_general(cotangent, lowrank_factor_second, (((1,), (1,)), ((), ())), preferred_element_type=jnp.float32).astype(jnp.bfloat16)
    grad_a = lax.dot_general(hidden_activation, cotangent_lowrank, (((0,), (0,)), ((), ())), preferred_element_type=jnp.float32)
    grad_b = lax.dot_general(lowrank_projection, cotangent.astype(jnp.float32), (((0,), (0,)), ((), ())), precision=lax.Precision.HIGHEST)
    cot_cols = cotangent.reshape(TOKENS, N_DP, per_col, BS).astype(jnp.float32)
    cot_pick = jnp.einsum("tond,ojkn->tojkd", cot_cols, col_pick, precision=lax.Precision.HIGHEST)
    grad_blocks = jnp.einsum("tojkc,tojkd->ojkcd", picked, cot_pick, precision=lax.Precision.HIGHEST)
    grad_blocks = grad_blocks * live[..., None, None]
    return (mixed, grad_a, grad_b, grad_blocks)
```

```python
import jax
import jax.numpy as jnp
from jax import lax
from jax.sharding import PartitionSpec as P


def shards(gate, up, cotangent, down_weight, factor_a, factor_b, blocks, slot_rows, slot_cols, counts):
    f32, bf16 = jnp.float32, jnp.bfloat16
    n_dp = lax.axis_size("dp")
    me = lax.axis_index("dp")
    tok_local, quarter = gate.shape
    width = down_weight.shape[1]
    rank = factor_a.shape[1]
    side = blocks.shape[-1]
    slots = blocks.shape[2]
    per_col = width // side
    hidden = (jax.nn.silu(gate.astype(f32)) * up.astype(f32)).astype(bf16)
    cot_low = lax.dot_general(
        cotangent, factor_b, (((1,), (1,)), ((), ())), preferred_element_type=f32
    ).astype(bf16)
    packed = jnp.concatenate([hidden, cot_low, jnp.zeros_like(cot_low)], axis=1)
    packed_all = lax.all_gather(packed, "dp", axis=0, tiled=True)
    hidden_all = packed_all[:, :quarter]
    cot_low_all = packed_all[:, quarter : quarter + rank]
    tok_all = tok_local * n_dp
    cot_cols = lax.all_to_all(
        cotangent.reshape(tok_local, n_dp, width), "dp", split_axis=1, concat_axis=0, tiled=True
    ).reshape(tok_all, width)
    rows = lax.dynamic_index_in_dim(slot_rows[:, 0, :], me, 0, keepdims=False)
    cols = lax.dynamic_index_in_dim(slot_cols[:, 0, :], me, 0, keepdims=False)
    live = jnp.arange(slots, dtype=jnp.int32) < lax.dynamic_index_in_dim(
        counts[:, 0], me, 0, keepdims=False
    )
    b_window = lax.dynamic_slice_in_dim(factor_b, me * width, width, 1).astype(f32)
    low = jnp.dot(hidden_all, factor_a, preferred_element_type=f32)
    total = jnp.dot(hidden_all, down_weight, preferred_element_type=f32)
    total = total + jnp.dot(low, b_window, precision=lax.Precision.HIGHEST)
    owned_h = [
        lax.dynamic_slice_in_dim(hidden_all, rows[s] * side, side, 1) for s in range(slots)
    ]
    owned_c = [
        lax.dynamic_slice_in_dim(cot_cols, cols[s] * side, side, 1) for s in range(slots)
    ]
    lanes = jnp.arange(per_col, dtype=jnp.int32)
    for s in range(slots):
        piece = jnp.dot(owned_h[s], blocks[0, 0, s], preferred_element_type=f32)
        pick = (lanes == cols[s]) & live[s]
        total = total + jnp.where(
            pick[None, :, None], piece[:, None, :], 0.0
        ).reshape(tok_all, width)
    mixed = lax.psum_scatter(total, "tensor", scatter_dimension=0, tiled=True).astype(bf16)
    low_parts = lax.all_gather(low, "tensor", axis=0)
    low_sum = jnp.sum(low_parts, axis=0)
    grad_b = lax.dot_general(
        low_sum,
        cot_cols.astype(f32),
        (((0,), (0,)), ((), ())),
        precision=lax.Precision.HIGHEST,
    )
    grad_a = lax.dot_general(
        hidden_all, cot_low_all, (((0,), (0,)), ((), ())), preferred_element_type=f32
    )
    grad_blocks = jnp.stack(
        [
            jnp.where(
                live[s],
                lax.dot_general(
                    owned_h[s],
                    owned_c[s],
                    (((0,), (0,)), ((), ())),
                    preferred_element_type=f32,
                ),
                0.0,
            )
            for s in range(slots)
        ]
    )[None, None]
    return (mixed, grad_a, grad_b, grad_blocks)


def solution(mesh):
    return jax.shard_map(
        shards,
        mesh=mesh,
        in_specs=(
            P("dp", "tensor"),
            P("dp", "tensor"),
            P("dp", None),
            P("tensor", "dp"),
            P("tensor", None),
            P(),
            P("dp", "tensor", None, None, None),
            P(None, "tensor", None),
            P(None, "tensor", None),
            P(None, "tensor"),
        ),
        out_specs=(
            P("tensor", "dp"),
            P("tensor", None),
            P(None, "dp"),
            P("dp", "tensor", None, None, None),
        ),
        check_vma=False,
    )
```

```python
import functools

import jax
import jax.numpy as jnp
from jax import lax
from jax.experimental import pallas as pl
from jax.experimental.pallas import tpu as pltpu
from jax.sharding import PartitionSpec as P

MESH = pl.DeviceIdType.MESH
F32, BF16 = jnp.float32, jnp.bfloat16
WEIGHT_PARTS = 4


def ring_place(index, n):
    odd, pair = lax.rem(index, 2), lax.div(index, 2)
    return (1 - odd) * pair + odd * (n - 1 - pair)


def ring_index(place, n):
    back = lax.div(place, n // 2)
    return (1 - back) * 2 * place + back * (2 * (n - 1 - place) + 1)


def gather_kernel(
    n, gate, up, cot, w_hbm, a_hbm, b_hbm,
    hid, cots, lows, total, low,
    w, a, b, cl,
    w_sem, ab_sem, ring_send, ring_recv, cot_send, cot_recv, cl_send, cl_recv,
):
    me = lax.axis_index("dp")
    tok, quarter = gate.shape
    width = cots.shape[1]
    rank = b.shape[0]
    part = quarter // WEIGHT_PARTS
    loads = [pltpu.make_async_copy(b_hbm, b, ab_sem.at[0])]
    loads += [
        pltpu.make_async_copy(
            w_hbm.at[pl.ds(i * part, part)], w.at[pl.ds(i * part, part)], w_sem.at[i]
        )
        for i in range(WEIGHT_PARTS)
    ]
    loads.append(pltpu.make_async_copy(a_hbm, a, ab_sem.at[1]))
    for load in loads:
        load.start()

    barrier = pltpu.get_barrier_semaphore()

    @pl.loop(1, n)
    def _(d):
        pl.semaphore_signal(
            barrier, inc=1, device_id={"dp": lax.rem(me + d, n)}, device_id_type=MESH
        )

    def rows(index):
        return pl.ds(pl.multiple_of(index * tok, tok), tok)

    mine = rows(me)
    half = quarter // 2
    step = 512

    @pl.loop(0, quarter // step)
    def _(i):
        at = pl.ds(pl.multiple_of(i * step, step), step)
        g = gate[:, at].astype(F32)
        hid[mine, at] = (g * jax.nn.sigmoid(g) * up[:, at].astype(F32)).astype(BF16)

    pl.semaphore_wait(barrier, n - 1)

    place = ring_place(me, n)
    right = ring_index(lax.rem(place + 1, n), n)
    left = ring_index(lax.rem(place + n - 1, n), n)
    streams = ((0, 1, n // 2), (1, -1, n // 2), (1, 1, n // 2 - 1), (0, -1, n // 2 - 1))

    def hop(k, s):
        which, way, _ = streams[k]
        slot = rows(ring_index(lax.rem(place - way * s + n, n), n))
        ref = hid.at[slot, pl.ds(which * half, half)]
        return pltpu.make_async_remote_copy(
            src_ref=ref,
            dst_ref=ref,
            send_sem=ring_send.at[k, s],
            recv_sem=ring_recv.at[k, s],
            device_id={"dp": right if way > 0 else left},
            device_id_type=MESH,
        )

    hops = {}

    def start(k, s):
        hops[k, s] = hop(k, s)
        hops[k, s].start()

    for k in range(4):
        start(k, 0)

    def cot_copy(d):
        peer = lax.rem(me + d, n)
        return pltpu.make_async_remote_copy(
            src_ref=cot.at[:, pl.ds(pl.multiple_of(peer * width, width), width)],
            dst_ref=cots.at[mine],
            send_sem=cot_send.at[d],
            recv_sem=cot_recv.at[d],
            device_id={"dp": peer},
            device_id_type=MESH,
        )

    def cl_copy(d):
        return pltpu.make_async_remote_copy(
            src_ref=cl,
            dst_ref=lows.at[mine],
            send_sem=cl_send.at[d],
            recv_sem=cl_recv.at[d],
            device_id={"dp": lax.rem(me + d, n)},
            device_id_type=MESH,
        )

    @pl.loop(1, n)
    def _(d):
        cot_copy(d).start()

    cots[mine] = cot[:, pl.ds(pl.multiple_of(me * width, width), width)]
    loads[0].wait()
    acc = jnp.zeros((tok, rank), F32)
    deep = cot.shape[1] // 8
    for i in range(8):
        acc += lax.dot_general(
            cot[:, i * deep : (i + 1) * deep],
            b[:, i * deep : (i + 1) * deep],
            (((1,), (1,)), ((), ())),
            preferred_element_type=F32,
        )
    cl[...] = jnp.concatenate([acc, jnp.zeros((tok, cl.shape[1] - rank), F32)], axis=1).astype(BF16)
    lows[mine] = cl[...]

    @pl.loop(1, n)
    def _(d):
        cl_copy(d).start()

    for s in range(n // 2):
        for k in range(4):
            if s < streams[k][2]:
                hops[k, s].wait_recv()
                if s + 1 < streams[k][2]:
                    start(k, s + 1)

    for load in loads[1:]:
        load.wait()
    total[...] = jnp.zeros_like(total)
    low[...] = jnp.zeros_like(low)
    tall = 1024

    @pl.loop(0, quarter // tall)
    def _(i):
        at = pl.ds(pl.multiple_of(i * tall, tall), tall)
        h = hid[:, at]
        total[...] += jnp.dot(h, w[at], preferred_element_type=F32)
        low[...] += jnp.dot(h, a[at], preferred_element_type=F32)

    for one in hops.values():
        one.wait_send()

    @pl.loop(1, n)
    def _(d):
        cot_copy(d).wait()
        cl_copy(d).wait()


def gather_and_multiply(gate, up, cotangent, down_weight, factor_a, factor_b):
    n = lax.axis_size("dp")
    tok, quarter = gate.shape
    width = down_weight.shape[1]
    rank = factor_a.shape[1]
    everyone = tok * n
    vmem = pl.BlockSpec(memory_space=pltpu.VMEM)
    anywhere = pl.BlockSpec(memory_space=pl.ANY)
    dma = pltpu.SemaphoreType.DMA
    return pl.pallas_call(
        functools.partial(gather_kernel, n),
        out_shape=(
            jax.ShapeDtypeStruct((everyone, quarter), BF16),
            jax.ShapeDtypeStruct((everyone, width), BF16),
            jax.ShapeDtypeStruct((everyone, 128), BF16),
            jax.ShapeDtypeStruct((everyone, width), F32),
            jax.ShapeDtypeStruct((everyone, rank), F32),
        ),
        in_specs=[vmem, vmem, vmem, anywhere, anywhere, anywhere],
        out_specs=[vmem] * 5,
        scratch_shapes=[
            pltpu.VMEM(down_weight.shape, BF16),
            pltpu.VMEM(factor_a.shape, BF16),
            pltpu.VMEM(factor_b.shape, BF16),
            pltpu.VMEM((tok, 128), BF16),
            dma((WEIGHT_PARTS,)),
            dma((2,)),
            dma((4, n // 2)),
            dma((4, n // 2)),
            dma((n,)),
            dma((n,)),
            dma((n,)),
            dma((n,)),
        ],
        compiler_params=pltpu.CompilerParams(
            collective_id=0, has_side_effects=True, vmem_limit_bytes=48 << 20
        ),
        name="gather_multiply",
    )(gate, up, cotangent, down_weight, factor_a, factor_b)


def shards(gate, up, cotangent, down_weight, factor_a, factor_b, blocks, slot_rows, slot_cols, counts):
    f32, bf16 = jnp.float32, jnp.bfloat16
    n_dp = lax.axis_size("dp")
    me = lax.axis_index("dp")
    tok_local = gate.shape[0]
    width = down_weight.shape[1]
    rank = factor_a.shape[1]
    side = blocks.shape[-1]
    slots = blocks.shape[2]
    per_col = width // side
    hidden_all, cot_cols, cot_low_all, total, low = gather_and_multiply(
        gate, up, cotangent, down_weight, factor_a, factor_b
    )
    cot_low_all = cot_low_all[:, :rank]
    tok_all = tok_local * n_dp
    rows = lax.dynamic_index_in_dim(slot_rows[:, 0, :], me, 0, keepdims=False)
    cols = lax.dynamic_index_in_dim(slot_cols[:, 0, :], me, 0, keepdims=False)
    live = jnp.arange(slots, dtype=jnp.int32) < lax.dynamic_index_in_dim(
        counts[:, 0], me, 0, keepdims=False
    )
    b_window = lax.dynamic_slice_in_dim(factor_b, me * width, width, 1).astype(f32)
    total = total + jnp.dot(low, b_window, precision=lax.Precision.HIGHEST)
    owned_h = [
        lax.dynamic_slice_in_dim(hidden_all, rows[s] * side, side, 1) for s in range(slots)
    ]
    owned_c = [
        lax.dynamic_slice_in_dim(cot_cols, cols[s] * side, side, 1) for s in range(slots)
    ]
    lanes = jnp.arange(per_col, dtype=jnp.int32)
    for s in range(slots):
        piece = jnp.dot(owned_h[s], blocks[0, 0, s], preferred_element_type=f32)
        pick = (lanes == cols[s]) & live[s]
        total = total + jnp.where(
            pick[None, :, None], piece[:, None, :], 0.0
        ).reshape(tok_all, width)
    mixed = lax.psum_scatter(total, "tensor", scatter_dimension=0, tiled=True).astype(bf16)
    low_parts = lax.all_gather(low, "tensor", axis=0)
    low_sum = jnp.sum(low_parts, axis=0)
    grad_b = lax.dot_general(
        low_sum,
        cot_cols.astype(f32),
        (((0,), (0,)), ((), ())),
        precision=lax.Precision.HIGHEST,
    )
    grad_a = lax.dot_general(
        hidden_all, cot_low_all, (((0,), (0,)), ((), ())), preferred_element_type=f32
    )
    grad_blocks = jnp.stack(
        [
            jnp.where(
                live[s],
                lax.dot_general(
                    owned_h[s],
                    owned_c[s],
                    (((0,), (0,)), ((), ())),
                    preferred_element_type=f32,
                ),
                0.0,
            )
            for s in range(slots)
        ]
    )[None, None]
    return (mixed, grad_a, grad_b, grad_blocks)


def solution(mesh):
    return jax.shard_map(
        shards,
        mesh=mesh,
        in_specs=(
            P("dp", "tensor"),
            P("dp", "tensor"),
            P("dp", None),
            P("tensor", "dp"),
            P("tensor", None),
            P(),
            P("dp", "tensor", None, None, None),
            P(None, "tensor", None),
            P(None, "tensor", None),
            P(None, "tensor"),
        ),
        out_specs=(
            P("tensor", "dp"),
            P("tensor", None),
            P(None, "dp"),
            P("dp", "tensor", None, None, None),
        ),
        check_vma=False,
    )
```

```python
import functools

import jax
import jax.numpy as jnp
from jax import lax
from jax.experimental import pallas as pl
from jax.experimental.pallas import tpu as pltpu
from jax.sharding import PartitionSpec as P

MESH = pl.DeviceIdType.MESH
F32, BF16 = jnp.float32, jnp.bfloat16
WEIGHT_PARTS = 4


def ring_place(index, n):
    odd, pair = lax.rem(index, 2), lax.div(index, 2)
    return (1 - odd) * pair + odd * (n - 1 - pair)


def ring_index(place, n):
    back = lax.div(place, n // 2)
    return (1 - back) * 2 * place + back * (2 * (n - 1 - place) + 1)


def gather_kernel(
    n, n_tensor, gate, up, cot, w_hbm, a_hbm, b_hbm, blocks, slot_rows, slot_cols, counts,
    hid, lows, mixed, grad_b, grad_blocks,
    w, a, b, cl, cots, total, parts, low_parts,
    w_sem, ab_sem, ring_send, ring_recv, cot_send, cot_recv, cl_send, cl_recv,
    low_send, low_recv, part_send, part_recv,
):
    me = lax.axis_index("dp")
    tok, quarter = gate.shape
    width = cots.shape[1]
    rank = b.shape[0]
    part = quarter // WEIGHT_PARTS
    loads = [pltpu.make_async_copy(b_hbm, b, ab_sem.at[0])]
    loads += [
        pltpu.make_async_copy(
            w_hbm.at[pl.ds(i * part, part)], w.at[pl.ds(i * part, part)], w_sem.at[i]
        )
        for i in range(WEIGHT_PARTS)
    ]
    loads.append(pltpu.make_async_copy(a_hbm, a, ab_sem.at[1]))
    for load in loads:
        load.start()

    barrier = pltpu.get_barrier_semaphore()

    @pl.loop(1, n)
    def _(d):
        pl.semaphore_signal(
            barrier, inc=1, device_id={"dp": lax.rem(me + d, n)}, device_id_type=MESH
        )

    mine_t = lax.axis_index("tensor")
    for d in range(1, n_tensor):
        pl.semaphore_signal(
            barrier,
            inc=1,
            device_id={"tensor": lax.rem(mine_t + d, n_tensor)},
            device_id_type=MESH,
        )

    def rows(index):
        return pl.ds(pl.multiple_of(index * tok, tok), tok)

    mine = rows(me)
    half = quarter // 2
    step = 512

    @pl.loop(0, quarter // step)
    def _(i):
        at = pl.ds(pl.multiple_of(i * step, step), step)
        g = gate[:, at].astype(F32)
        hid[mine, at] = (g * jax.nn.sigmoid(g) * up[:, at].astype(F32)).astype(BF16)

    pl.semaphore_wait(barrier, n - 1 + n_tensor - 1)

    place = ring_place(me, n)
    right = ring_index(lax.rem(place + 1, n), n)
    left = ring_index(lax.rem(place + n - 1, n), n)
    streams = ((0, 1, n // 2), (1, -1, n // 2), (1, 1, n // 2 - 1), (0, -1, n // 2 - 1))

    def hop(k, s):
        which, way, _ = streams[k]
        slot = rows(ring_index(lax.rem(place - way * s + n, n), n))
        ref = hid.at[slot, pl.ds(which * half, half)]
        return pltpu.make_async_remote_copy(
            src_ref=ref,
            dst_ref=ref,
            send_sem=ring_send.at[k, s],
            recv_sem=ring_recv.at[k, s],
            device_id={"dp": right if way > 0 else left},
            device_id_type=MESH,
        )

    hops = {}

    def start(k, s):
        hops[k, s] = hop(k, s)
        hops[k, s].start()

    for k in range(4):
        start(k, 0)

    def cot_copy(d):
        peer = lax.rem(me + d, n)
        return pltpu.make_async_remote_copy(
            src_ref=cot.at[:, pl.ds(pl.multiple_of(peer * width, width), width)],
            dst_ref=cots.at[mine],
            send_sem=cot_send.at[d],
            recv_sem=cot_recv.at[d],
            device_id={"dp": peer},
            device_id_type=MESH,
        )

    def cl_copy(d):
        return pltpu.make_async_remote_copy(
            src_ref=cl,
            dst_ref=lows.at[mine],
            send_sem=cl_send.at[d],
            recv_sem=cl_recv.at[d],
            device_id={"dp": lax.rem(me + d, n)},
            device_id_type=MESH,
        )

    @pl.loop(1, n)
    def _(d):
        cot_copy(d).start()

    cots[mine] = cot[:, pl.ds(pl.multiple_of(me * width, width), width)]
    loads[0].wait()
    acc = jnp.zeros((tok, rank), F32)
    deep = cot.shape[1] // 8
    for i in range(8):
        acc += lax.dot_general(
            cot[:, i * deep : (i + 1) * deep],
            b[:, i * deep : (i + 1) * deep],
            (((1,), (1,)), ((), ())),
            preferred_element_type=F32,
        )
    cl[...] = jnp.concatenate([acc, jnp.zeros((tok, cl.shape[1] - rank), F32)], axis=1).astype(BF16)
    lows[mine] = cl[...]

    @pl.loop(1, n)
    def _(d):
        cl_copy(d).start()

    for s in range(n // 2):
        for k in range(4):
            if s < streams[k][2]:
                hops[k, s].wait_recv()
                if s + 1 < streams[k][2]:
                    start(k, s + 1)

    for load in loads[1:]:
        load.wait()
    tall = 1024
    spread = quarter // tall
    low = jnp.zeros((total.shape[0], rank), F32)
    for i in range(spread):
        at = slice(i * tall, (i + 1) * tall)
        low += lax.dot_general(
            hid[:, at], a[:, at], (((1,), (1,)), ((), ())), preferred_element_type=F32
        )
    low_parts[mine_t] = jnp.concatenate(
        [low, jnp.zeros((low.shape[0], low_parts.shape[2] - rank), F32)], axis=1
    )

    def low_copy(d):
        return pltpu.make_async_remote_copy(
            src_ref=low_parts.at[mine_t],
            dst_ref=low_parts.at[mine_t],
            send_sem=low_send.at[d],
            recv_sem=low_recv.at[d],
            device_id={"tensor": lax.rem(mine_t + d, n_tensor)},
            device_id_type=MESH,
        )

    share = mixed.shape[0]

    def part_copy(d):
        peer = lax.rem(mine_t + d, n_tensor)
        return pltpu.make_async_remote_copy(
            src_ref=total.at[pl.ds(pl.multiple_of(peer * share, share), share)],
            dst_ref=parts.at[mine_t],
            send_sem=part_send.at[d],
            recv_sem=part_recv.at[d],
            device_id={"tensor": peer},
            device_id_type=MESH,
        )

    for d in range(1, n_tensor):
        low_copy(d).start()

    window = b[:, pl.ds(pl.multiple_of(me * width, width), width)].astype(F32)
    total[...] = jnp.dot(low, window, precision=lax.Precision.HIGHEST, preferred_element_type=F32)
    side = blocks.shape[-1]
    slots = blocks.shape[0]

    square = (hid.shape[0], side)

    def owned(ref, block):
        name = jnp.full(square, block, jnp.int32)

        def look(r, kept):
            here = ref[:, pl.ds(pl.multiple_of(r * side, side), side)].astype(F32)
            return jnp.where(name == r, here, kept)

        found = lax.fori_loop(0, ref.shape[1] // side, look, jnp.zeros(square, F32))
        return found.astype(BF16)

    live = jnp.full((8, side), counts[me, 0], jnp.int32)
    held = [owned(hid, slot_rows[me, k]) for k in range(slots)]
    for k in range(slots):
        piece = jnp.dot(held[k], blocks[k], preferred_element_type=F32)
        column = jnp.full((8, side), slot_cols[me, k], jnp.int32)
        for c in range(width // side):
            on = jnp.where((column == c) & (live > k), 1.0, 0.0)[:1]
            total[:, c * side : (c + 1) * side] += piece * on

    @pl.loop(0, spread)
    def _(i):
        at = pl.ds(pl.multiple_of(i * tall, tall), tall)
        total[...] += jnp.dot(hid[:, at], w[at], preferred_element_type=F32)

    for d in range(1, n_tensor):
        part_copy(d).start()
    parts[mine_t] = total[pl.ds(pl.multiple_of(mine_t * share, share), share)]

    @pl.loop(1, n)
    def _(d):
        cot_copy(d).wait()
        cl_copy(d).wait()

    for k in range(slots):
        block = lax.dot_general(
            held[k],
            owned(cots, slot_cols[me, k]),
            (((0,), (0,)), ((), ())),
            preferred_element_type=F32,
        )
        grad_blocks[k] = block * jnp.where(live > k, 1.0, 0.0)[:1]

    for d in range(1, n_tensor):
        low_copy(d).wait()
    low_sum = low_parts[0]
    for i in range(1, n_tensor):
        low_sum += low_parts[i]
    grad_b[...] = jnp.dot(
        low_sum.T[:rank],
        cots[...].astype(F32),
        precision=lax.Precision.HIGHEST,
        preferred_element_type=F32,
    )

    for d in range(1, n_tensor):
        part_copy(d).wait()
    whole = parts[0]
    for i in range(1, n_tensor):
        whole += parts[i]
    mixed[...] = whole.astype(BF16)

    for one in hops.values():
        one.wait_send()


def gather_and_multiply(
    gate, up, cotangent, down_weight, factor_a, factor_b, blocks, slot_rows, slot_cols, counts
):
    n_tensor = lax.axis_size("tensor")
    n = lax.axis_size("dp")
    tok, quarter = gate.shape
    width = down_weight.shape[1]
    rank = factor_a.shape[0]
    everyone = tok * n
    vmem = pl.BlockSpec(memory_space=pltpu.VMEM)
    anywhere = pl.BlockSpec(memory_space=pl.ANY)
    dma = pltpu.SemaphoreType.DMA
    return pl.pallas_call(
        functools.partial(gather_kernel, n, n_tensor),
        out_shape=(
            jax.ShapeDtypeStruct((everyone, quarter), BF16),
            jax.ShapeDtypeStruct((everyone, 128), BF16),
            jax.ShapeDtypeStruct((everyone // n_tensor, width), BF16),
            jax.ShapeDtypeStruct((rank, width), F32),
            jax.ShapeDtypeStruct(blocks.shape, F32),
        ),
        in_specs=[vmem] * 3 + [anywhere] * 3 + [vmem] + [pl.BlockSpec(memory_space=pltpu.SMEM)] * 3,
        out_specs=[vmem] * 5,
        scratch_shapes=[
            pltpu.VMEM(down_weight.shape, BF16),
            pltpu.VMEM(factor_a.shape, BF16),
            pltpu.VMEM(factor_b.shape, BF16),
            pltpu.VMEM((tok, 128), BF16),
            pltpu.VMEM((everyone, width), BF16),
            pltpu.VMEM((everyone, width), F32),
            pltpu.VMEM((n_tensor, everyone // n_tensor, width), F32),
            pltpu.VMEM((n_tensor, everyone, 128), F32),
            dma((WEIGHT_PARTS,)),
            dma((2,)),
            dma((4, n // 2)),
            dma((4, n // 2)),
            dma((n,)),
            dma((n,)),
            dma((n,)),
            dma((n,)),
            dma((n_tensor,)),
            dma((n_tensor,)),
            dma((n_tensor,)),
            dma((n_tensor,)),
        ],
        compiler_params=pltpu.CompilerParams(
            collective_id=0, has_side_effects=True, vmem_limit_bytes=48 << 20
        ),
        name="gather_multiply",
    )(
        gate, up, cotangent, down_weight, factor_a, factor_b, blocks, slot_rows, slot_cols, counts
    )


def shards(gate, up, cotangent, down_weight, factor_a, factor_b, blocks, slot_rows, slot_cols, counts):
    rank = factor_a.shape[1]
    hidden_all, cot_low_all, mixed, grad_b, grad_blocks = gather_and_multiply(
        gate,
        up,
        cotangent,
        down_weight,
        factor_a.T,
        factor_b,
        blocks[0, 0],
        slot_rows[:, 0, :],
        slot_cols[:, 0, :],
        counts,
    )
    grad_a = lax.dot_general(
        hidden_all,
        cot_low_all[:, :rank],
        (((0,), (0,)), ((), ())),
        preferred_element_type=F32,
    )
    return (mixed, grad_a, grad_b, grad_blocks[None, None])


def solution(mesh):
    return jax.shard_map(
        shards,
        mesh=mesh,
        in_specs=(
            P("dp", "tensor"),
            P("dp", "tensor"),
            P("dp", None),
            P("tensor", "dp"),
            P("tensor", None),
            P(),
            P("dp", "tensor", None, None, None),
            P(None, "tensor", None),
            P(None, "tensor", None),
            P(None, "tensor"),
        ),
        out_specs=(
            P("tensor", "dp"),
            P("tensor", None),
            P(None, "dp"),
            P("dp", "tensor", None, None, None),
        ),
        check_vma=False,
    )
```

```python
import functools

import jax
import jax.numpy as jnp
from jax import lax
from jax.experimental import pallas as pl
from jax.experimental.pallas import tpu as pltpu
from jax.sharding import PartitionSpec as P

MESH = pl.DeviceIdType.MESH
F32, BF16 = jnp.float32, jnp.bfloat16
WEIGHT_PARTS = 4


def ring_place(index, n):
    odd, pair = lax.rem(index, 2), lax.div(index, 2)
    return (1 - odd) * pair + odd * (n - 1 - pair)


def ring_index(place, n):
    back = lax.div(place, n // 2)
    return (1 - back) * 2 * place + back * (2 * (n - 1 - place) + 1)


def gather_kernel(
    n, n_tensor, gate, up, cot, w_hbm, a_hbm, b_hbm, blocks, slot_rows, slot_cols, counts,
    hid, lows, mixed, grad_b, grad_blocks,
    w, a, b, cl, cots, total, parts, low_parts,
    w_sem, ab_sem, ring_send, ring_recv, cot_send, cot_recv, cl_send, cl_recv,
    low_send, low_recv, part_send, part_recv,
):
    me = lax.axis_index("dp")
    tok, quarter = gate.shape
    width = cots.shape[1]
    rank = b.shape[0]
    part = quarter // WEIGHT_PARTS
    loads = [pltpu.make_async_copy(b_hbm, b, ab_sem.at[0])]
    loads += [
        pltpu.make_async_copy(
            w_hbm.at[pl.ds(i * part, part)], w.at[pl.ds(i * part, part)], w_sem.at[i]
        )
        for i in range(WEIGHT_PARTS)
    ]
    loads.append(pltpu.make_async_copy(a_hbm, a, ab_sem.at[1]))
    for load in loads:
        load.start()

    barrier = pltpu.get_barrier_semaphore()

    @pl.loop(1, n)
    def _(d):
        pl.semaphore_signal(
            barrier, inc=1, device_id={"dp": lax.rem(me + d, n)}, device_id_type=MESH
        )

    mine_t = lax.axis_index("tensor")
    for d in range(1, n_tensor):
        pl.semaphore_signal(
            barrier,
            inc=1,
            device_id={"tensor": lax.rem(mine_t + d, n_tensor)},
            device_id_type=MESH,
        )

    def rows(index):
        return pl.ds(pl.multiple_of(index * tok, tok), tok)

    mine = rows(me)
    half = quarter // 2
    step = 512

    @pl.loop(0, quarter // step)
    def _(i):
        at = pl.ds(pl.multiple_of(i * step, step), step)
        g = gate[:, at].astype(F32)
        hid[mine, at] = (g * jax.nn.sigmoid(g) * up[:, at].astype(F32)).astype(BF16)

    pl.semaphore_wait(barrier, n - 1 + n_tensor - 1)

    place = ring_place(me, n)
    right = ring_index(lax.rem(place + 1, n), n)
    left = ring_index(lax.rem(place + n - 1, n), n)
    streams = ((0, 1, n // 2), (1, -1, n // 2), (1, 1, n // 2 - 1), (0, -1, n // 2 - 1))

    def hop(k, s):
        which, way, _ = streams[k]
        slot = rows(ring_index(lax.rem(place - way * s + n, n), n))
        ref = hid.at[slot, pl.ds(which * half, half)]
        return pltpu.make_async_remote_copy(
            src_ref=ref,
            dst_ref=ref,
            send_sem=ring_send.at[k, s],
            recv_sem=ring_recv.at[k, s],
            device_id={"dp": right if way > 0 else left},
            device_id_type=MESH,
        )

    hops = {}

    def start(k, s):
        hops[k, s] = hop(k, s)
        hops[k, s].start()

    for k in range(4):
        start(k, 0)

    def cot_copy(d):
        peer = lax.rem(me + d, n)
        return pltpu.make_async_remote_copy(
            src_ref=cot.at[:, pl.ds(pl.multiple_of(peer * width, width), width)],
            dst_ref=cots.at[mine],
            send_sem=cot_send.at[d],
            recv_sem=cot_recv.at[d],
            device_id={"dp": peer},
            device_id_type=MESH,
        )

    def cl_copy(d):
        return pltpu.make_async_remote_copy(
            src_ref=cl,
            dst_ref=lows.at[mine],
            send_sem=cl_send.at[d],
            recv_sem=cl_recv.at[d],
            device_id={"dp": lax.rem(me + d, n)},
            device_id_type=MESH,
        )

    @pl.loop(1, n)
    def _(d):
        cot_copy(d).start()

    cots[mine] = cot[:, pl.ds(pl.multiple_of(me * width, width), width)]
    loads[0].wait()
    acc = jnp.zeros((tok, rank), F32)
    deep = cot.shape[1] // 8
    for i in range(8):
        acc += lax.dot_general(
            cot[:, i * deep : (i + 1) * deep],
            b[:, i * deep : (i + 1) * deep],
            (((1,), (1,)), ((), ())),
            preferred_element_type=F32,
        )
    cl[...] = jnp.concatenate([acc, jnp.zeros((tok, cl.shape[1] - rank), F32)], axis=1).astype(BF16)
    lows[mine] = cl[...]

    @pl.loop(1, n)
    def _(d):
        cl_copy(d).start()

    for s in range(n // 2):
        for k in range(4):
            if s < streams[k][2]:
                hops[k, s].wait_recv()
                if s + 1 < streams[k][2]:
                    start(k, s + 1)

    for load in loads[1:]:
        load.wait()
    tall = 1024
    spread = quarter // tall
    low = jnp.zeros((total.shape[0], rank), F32)
    for i in range(spread):
        at = slice(i * tall, (i + 1) * tall)
        low += lax.dot_general(
            hid[:, at], a[:, at], (((1,), (1,)), ((), ())), preferred_element_type=F32
        )
    low_parts[mine_t] = jnp.concatenate(
        [low, jnp.zeros((low.shape[0], low_parts.shape[2] - rank), F32)], axis=1
    )

    def low_copy(d):
        return pltpu.make_async_remote_copy(
            src_ref=low_parts.at[mine_t],
            dst_ref=low_parts.at[mine_t],
            send_sem=low_send.at[d],
            recv_sem=low_recv.at[d],
            device_id={"tensor": lax.rem(mine_t + d, n_tensor)},
            device_id_type=MESH,
        )

    share = mixed.shape[0]

    def part_copy(d):
        peer = lax.rem(mine_t + d, n_tensor)
        return pltpu.make_async_remote_copy(
            src_ref=total.at[pl.ds(pl.multiple_of(peer * share, share), share)],
            dst_ref=parts.at[mine_t],
            send_sem=part_send.at[d],
            recv_sem=part_recv.at[d],
            device_id={"tensor": peer},
            device_id_type=MESH,
        )

    for d in range(1, n_tensor):
        low_copy(d).start()

    window = b[:, pl.ds(pl.multiple_of(me * width, width), width)].astype(F32)
    total[...] = jnp.dot(low, window, precision=lax.Precision.HIGHEST, preferred_element_type=F32)
    side = blocks.shape[-1]
    slots = blocks.shape[0]

    square = (hid.shape[0], side)

    def owned(ref, block):
        name = jnp.full(square, block, jnp.int32)

        def look(r, kept):
            here = ref[:, pl.ds(pl.multiple_of(r * side, side), side)].astype(F32)
            return jnp.where(name == r, here, kept)

        found = lax.fori_loop(0, ref.shape[1] // side, look, jnp.zeros(square, F32))
        return found.astype(BF16)

    live = jnp.full((8, side), counts[me, 0], jnp.int32)
    held = [owned(hid, slot_rows[me, k]) for k in range(slots)]
    for k in range(slots):
        piece = jnp.dot(held[k], blocks[k], preferred_element_type=F32)
        column = jnp.full((8, side), slot_cols[me, k], jnp.int32)
        for c in range(width // side):
            on = jnp.where((column == c) & (live > k), 1.0, 0.0)[:1]
            total[:, c * side : (c + 1) * side] += piece * on

    @pl.loop(0, spread)
    def _(i):
        at = pl.ds(pl.multiple_of(i * tall, tall), tall)
        total[...] += jnp.dot(hid[:, at], w[at], preferred_element_type=F32)

    for d in range(1, n_tensor):
        part_copy(d).start()
    parts[mine_t] = total[pl.ds(pl.multiple_of(mine_t * share, share), share)]

    @pl.loop(1, n)
    def _(d):
        cot_copy(d).wait()
        cl_copy(d).wait()

    for k in range(slots):
        block = lax.dot_general(
            held[k],
            owned(cots, slot_cols[me, k]),
            (((0,), (0,)), ((), ())),
            preferred_element_type=F32,
        )
        grad_blocks[k] = block * jnp.where(live > k, 1.0, 0.0)[:1]

    for d in range(1, n_tensor):
        low_copy(d).wait()
    low_sum = low_parts[0]
    for i in range(1, n_tensor):
        low_sum += low_parts[i]
    grad_b[...] = jnp.dot(
        low_sum.T[:rank],
        cots[...].astype(F32),
        precision=lax.Precision.HIGHEST,
        preferred_element_type=F32,
    )

    for d in range(1, n_tensor):
        part_copy(d).wait()
    whole = parts[0]
    for i in range(1, n_tensor):
        whole += parts[i]
    mixed[...] = whole.astype(BF16)

    for one in hops.values():
        one.wait_send()


def gather_and_multiply(
    gate, up, cotangent, down_weight, factor_a, factor_b, blocks, slot_rows, slot_cols, counts
):
    n_tensor = lax.axis_size("tensor")
    n = lax.axis_size("dp")
    tok, quarter = gate.shape
    width = down_weight.shape[1]
    rank = factor_a.shape[0]
    everyone = tok * n
    vmem = pl.BlockSpec(memory_space=pltpu.VMEM)
    anywhere = pl.BlockSpec(memory_space=pltpu.HBM)
    dma = pltpu.SemaphoreType.DMA
    return pl.pallas_call(
        functools.partial(gather_kernel, n, n_tensor),
        out_shape=(
            jax.ShapeDtypeStruct((everyone, quarter), BF16),
            jax.ShapeDtypeStruct((everyone, 128), BF16),
            jax.ShapeDtypeStruct((everyone // n_tensor, width), BF16),
            jax.ShapeDtypeStruct((rank, width), F32),
            jax.ShapeDtypeStruct(blocks.shape, F32),
        ),
        in_specs=[vmem] * 3 + [anywhere] * 3 + [vmem] + [pl.BlockSpec(memory_space=pltpu.SMEM)] * 3,
        out_specs=[vmem] * 5,
        scratch_shapes=[
            pltpu.VMEM(down_weight.shape, BF16),
            pltpu.VMEM(factor_a.shape, BF16),
            pltpu.VMEM(factor_b.shape, BF16),
            pltpu.VMEM((tok, 128), BF16),
            pltpu.VMEM((everyone, width), BF16),
            pltpu.VMEM((everyone, width), F32),
            pltpu.VMEM((n_tensor, everyone // n_tensor, width), F32),
            pltpu.VMEM((n_tensor, everyone, 128), F32),
            dma((WEIGHT_PARTS,)),
            dma((2,)),
            dma((4, n // 2)),
            dma((4, n // 2)),
            dma((n,)),
            dma((n,)),
            dma((n,)),
            dma((n,)),
            dma((n_tensor,)),
            dma((n_tensor,)),
            dma((n_tensor,)),
            dma((n_tensor,)),
        ],
        compiler_params=pltpu.CompilerParams(
            collective_id=0, has_side_effects=True, vmem_limit_bytes=60 << 20
        ),
        name="gather_multiply",
    )(
        gate, up, cotangent, down_weight, factor_a, factor_b, blocks, slot_rows, slot_cols, counts
    )


def shards(gate, up, cotangent, down_weight, factor_a, factor_b, blocks, slot_rows, slot_cols, counts):
    rank = factor_a.shape[1]
    hidden_all, cot_low_all, mixed, grad_b, grad_blocks = gather_and_multiply(
        gate,
        up,
        cotangent,
        down_weight,
        factor_a.T,
        factor_b,
        blocks[0, 0],
        slot_rows[:, 0, :],
        slot_cols[:, 0, :],
        counts,
    )
    grad_a = lax.dot_general(
        hidden_all,
        cot_low_all[:, :rank],
        (((0,), (0,)), ((), ())),
        preferred_element_type=F32,
    )
    return (mixed, grad_a, grad_b, grad_blocks[None, None])


def solution(mesh):
    return jax.shard_map(
        shards,
        mesh=mesh,
        in_specs=(
            P("dp", "tensor"),
            P("dp", "tensor"),
            P("dp", None),
            P("tensor", "dp"),
            P("tensor", None),
            P(),
            P("dp", "tensor", None, None, None),
            P(None, "tensor", None),
            P(None, "tensor", None),
            P(None, "tensor"),
        ),
        out_specs=(
            P("tensor", "dp"),
            P("tensor", None),
            P(None, "dp"),
            P("dp", "tensor", None, None, None),
        ),
        check_vma=False,
    )
```
